128 devices in a mesh: gx: 8 (over y, core), gy: 16 (over x, z).
Axes of the slice: x: 4, y: 4, z: 4, core: 2. Of those that a mesh axis runs over, the one named last changes fastest.
Arguments:
- vectors: bfloat16 [32, 524288], P(None, ('gx', 'gy')), may hold values from -6 to 6
- near_tiles: bfloat16 [2048, 6, 256, 256], P(('gx', 'gy')), may hold values from -0.15625 to 0.15625
- near_list: int32 [2048, 6], P(('gx', 'gy')), may hold values from 0 to 2047, as said below
- leaf_basis: bfloat16 [2048, 64, 256], P(('gx', 'gy')), may hold values from -0.375 to 0.375
- leaf_transfer: bfloat16 [2048, 64, 64], P(('gx', 'gy')), may hold values from -0.1875 to 0.1875
- far_coupling: bfloat16 [2048, 24, 64, 64], P(('gx', 'gy')), may hold values from -0.15625 to 0.15625
- far_list: int32 [2048, 24], P(('gx', 'gy')), may hold values from 0 to 2047, as said below
- top_transfer: float32 [256, 64, 64], replicated, may hold values from -0.625 to 0.625
- top_coupling: float32 [256, 64, 64], replicated, may hold values from -0.75 to 0.75
Outputs:
- product: float32 [32, 524288], P(None, ('gx', 'gy'))
The draws below stay inside these ranges and needn't reach their ends.
Inputs may be any that keep to these rules, and one draw needn't show every extreme that they name: `near_list`: entry 0 of a leaf's list is the leaf itself; the others are distinct leaves whose grid positions differ from the leaf's by at most one along each dimension. `far_list`: the entries of one leaf are distinct leaves whose parent boxes differ from the leaf's parent box by at most one along each dimension, and whose grid positions differ from the leaf's by two or more along some dimension.
All inputs are finite; a program needn't handle non-finite values.
Results may differ from the reference program's by a relative error of at most 0.0023.
Values may be sent and summed in bfloat16 or wider, within the bound.
A program may use at most 192 MiB of HBM per device.

```python
import jax
import jax.numpy as jnp
from jax import lax

LEAF = 256
R = 64
VEC = 32
LEAF_DEV = 16
NB = 6
K_FAR = 24
NDEV = 128
GRID_X = 16
GRID_Y = 32
DEPTH = 4
TOPL = 7
LEAVES = 2048
POINTS = 524288


def place_of(leaf_index):
    device = leaf_index // LEAF_DEV
    inside = leaf_index % LEAF_DEV
    coord_x = 2 * (device // (GRID_Y // 2)) + inside % 2
    coord_y = 2 * (device % (GRID_Y // 2)) + inside // 2 % 2
    coord_z = inside // 4
    return (coord_x, coord_y, coord_z)


def leaf_at(coord_x, coord_y, coord_z):
    coord_x = jnp.clip(coord_x, 0, GRID_X - 1)
    coord_y = jnp.clip(coord_y, 0, GRID_Y - 1)
    coord_z = jnp.clip(coord_z, 0, DEPTH - 1)
    device = coord_x // 2 * (GRID_Y // 2) + coord_y // 2
    return (device * LEAF_DEV + coord_x % 2 + 2 * (coord_y % 2) + 4 * coord_z).astype(jnp.int32)


def inside_grid(coord_x, coord_y, coord_z):
    return (coord_x >= 0) & (coord_x < GRID_X) & (coord_y >= 0) & (coord_y < GRID_Y) & (coord_z >= 0) & (coord_z < DEPTH)


def draw_near_list(key, part):
    key = jax.random.fold_in(key, 5)
    leaf_ids = jnp.arange(LEAVES, dtype=jnp.int32)
    coord_x, coord_y, coord_z = place_of(leaf_ids)
    offset_code = jnp.arange(27, dtype=jnp.int32)
    shift_x = offset_code // 9 - 1
    shift_y = offset_code // 3 % 3 - 1
    shift_z = offset_code % 3 - 1
    near_x = coord_x[:, None] + shift_x[None, :]
    near_y = coord_y[:, None] + shift_y[None, :]
    near_z = coord_z[:, None] + shift_z[None, :]
    usable = inside_grid(near_x, near_y, near_z) & (offset_code != 13)[None, :]
    scores = jax.random.randint(key, (LEAVES, 27), 0, 1 << 20) * 32 + offset_code[None, :]
    scores = jnp.where(usable, scores, 1 << 30)
    ranked = jnp.argsort(scores, axis=1)[:, :NB - 1]
    candidates = leaf_at(near_x, near_y, near_z)
    picked = jnp.take_along_axis(candidates, ranked, axis=1)
    return jnp.concatenate([leaf_ids[:, None], picked], axis=1).astype(jnp.int32)


def draw_far_list(key, part):
    key = jax.random.fold_in(key, 11)
    leaf_ids = jnp.arange(LEAVES, dtype=jnp.int32)
    coord_x, coord_y, coord_z = place_of(leaf_ids)
    offset_code = jnp.arange(343, dtype=jnp.int32)
    shift_x = offset_code // 49 - 3
    shift_y = offset_code // 7 % 7 - 3
    shift_z = offset_code % 7 - 3
    far_x = coord_x[:, None] + shift_x[None, :]
    far_y = coord_y[:, None] + shift_y[None, :]
    far_z = coord_z[:, None] + shift_z[None, :]
    parent_near = (jnp.abs(jnp.clip(far_x, 0, GRID_X - 1) // 2 - coord_x[:, None] // 2) <= 1) & (jnp.abs(jnp.clip(far_y, 0, GRID_Y - 1) // 2 - coord_y[:, None] // 2) <= 1) & (jnp.abs(jnp.clip(far_z, 0, DEPTH - 1) // 2 - coord_z[:, None] // 2) <= 1)
    separated = jnp.maximum(jnp.maximum(jnp.abs(shift_x), jnp.abs(shift_y)), jnp.abs(shift_z)) >= 2
    usable = inside_grid(far_x, far_y, far_z) & parent_near & separated[None, :]
    scores = jax.random.randint(key, (LEAVES, 343), 0, 1 << 20) * 512 + offset_code[None, :]
    scores = jnp.where(usable, scores, 1 << 30)
    ranked = jnp.argsort(scores, axis=1)[:, :K_FAR]
    candidates = leaf_at(far_x, far_y, far_z)
    return jnp.take_along_axis(candidates, ranked, axis=1).astype(jnp.int32)


def levels(stream_key, dims, cuts, low, top_value):
    def one(axis_at, shards_of):
        draws = jax.random.uniform(jax.random.fold_in(jax.random.fold_in(stream_key, 6), axis_at), (shards_of,), jnp.float32, low / len(cuts), top_value / len(cuts))
        return jnp.repeat(jnp.exp(draws), dims[axis_at] // shards_of).reshape((-1,) + (1,) * (len(dims) - axis_at - 1))

    level = one(*cuts[0])
    for cut in cuts[1:]:
        level = level * one(*cut)
    return level


def gaussian(rng, extent, spread, limit, cuts=(), kind=jnp.bfloat16):
    gain = levels(rng, extent, cuts, -0.22, 0.18) if cuts else 1.0
    values = jax.random.normal(rng, extent, jnp.float32) * spread * gain
    return jnp.minimum(jnp.maximum(values, -limit), limit).astype(kind)


def setup_inputs(seed: int = 0) -> dict:
    arg_keys = jax.random.split(jax.random.key(seed), 10)
    vectors = gaussian(arg_keys[0], (VEC, POINTS), 1.0, 6.0, ((1, 128),))
    near_tiles = gaussian(arg_keys[1], (LEAVES, NB, LEAF, LEAF), (NB * LEAF) ** -0.5, 0.15625, ((0, 128),))
    near_list = draw_near_list(jax.random.fold_in(arg_keys[9], 71), 0)
    leaf_basis = gaussian(arg_keys[3], (LEAVES, R, LEAF), LEAF ** -0.5, 0.375, ((0, 128),))
    leaf_transfer = gaussian(arg_keys[4], (LEAVES, R, R), (R * LEAF_DEV) ** -0.5, 0.1875, ((0, 128),))
    far_coupling = gaussian(arg_keys[5], (LEAVES, K_FAR, R, R), (R * K_FAR) ** -0.5, 0.15625, ((0, 128),))
    far_list = draw_far_list(jax.random.fold_in(arg_keys[9], 71), 0)
    top_transfer = gaussian(arg_keys[7], (2 * NDEV, R, R), (3 * R // 2) ** -0.5, 0.625, (), jnp.float32)
    top_coupling = gaussian(arg_keys[8], (2 * NDEV, R, R), R ** -0.5, 0.75, (), jnp.float32)
    return dict(vectors=vectors, near_tiles=near_tiles, near_list=near_list, leaf_basis=leaf_basis, leaf_transfer=leaf_transfer, far_coupling=far_coupling, far_list=far_list, top_transfer=top_transfer, top_coupling=top_coupling)


def reference(vectors, near_tiles, near_list, leaf_basis, leaf_transfer, far_coupling, far_list, top_transfer, top_coupling):
    highest = lax.Precision.HIGHEST
    blocks = vectors.reshape(VEC, LEAVES, LEAF)
    moments = jnp.einsum('lrp,vlp->lrv', leaf_basis.astype(jnp.float32), blocks.astype(jnp.float32), precision=highest).astype(jnp.bfloat16)

    def near_leaf(inputs):
        tile_set, leaf_index = inputs
        pieces = jnp.take(blocks, leaf_index, axis=1).reshape(VEC, NB * LEAF)
        weights = jnp.transpose(tile_set, (0, 2, 1)).reshape(NB * LEAF, LEAF)
        return jnp.dot(pieces, weights, preferred_element_type=jnp.float32)

    near_field = lax.map(near_leaf, (near_tiles, near_list.astype(jnp.int32)))

    def far_leaf(inputs):
        coupling, leaf_index = inputs
        pieces = jnp.take(moments, leaf_index, axis=0)
        return jnp.einsum('krs,ksv->rv', coupling.astype(jnp.float32), pieces.astype(jnp.float32), precision=highest)

    far_field = lax.map(far_leaf, (far_coupling, far_list.astype(jnp.int32)))

    transfer_dev = leaf_transfer.reshape(NDEV, LEAF_DEV, R, R).astype(jnp.float32)
    box_moment = jnp.einsum('dlrs,dlsv->drv', transfer_dev, moments.reshape(NDEV, LEAF_DEV, R, VEC).astype(jnp.float32), precision=highest)
    moments_up = [box_moment]
    for height in range(TOPL - 1):
        box_count = NDEV >> height
        heap_index = box_count + jnp.arange(box_count, dtype=jnp.int32)
        carried = jnp.einsum('nrs,nsv->nrv', top_transfer[heap_index], moments_up[-1], precision=highest)
        moments_up.append(carried[0::2] + carried[1::2])
    local_top = None
    for height in reversed(range(TOPL)):
        box_count = NDEV >> height
        heap_index = box_count + jnp.arange(box_count, dtype=jnp.int32)
        sibling = moments_up[height][jnp.arange(box_count, dtype=jnp.int32) ^ 1]
        coupled = jnp.einsum('nrs,nsv->nrv', top_coupling[heap_index], sibling, precision=highest)
        if local_top is not None:
            coupled = coupled + jnp.einsum('nsr,nsv->nrv', top_transfer[heap_index], jnp.repeat(local_top, 2, axis=0), precision=highest)
        local_top = coupled
    from_box = jnp.einsum('dlrs,drv->dlsv', transfer_dev, local_top, precision=highest).reshape(LEAVES, R, VEC)
    local_coeffs = (far_field + from_box).astype(jnp.bfloat16)
    far_out = jnp.einsum('lrp,lrv->lvp', leaf_basis.astype(jnp.float32), local_coeffs.astype(jnp.float32), precision=highest)
    summed = near_field + far_out
    return jnp.transpose(summed, (1, 0, 2)).reshape(VEC, POINTS)
```

```python
import jax
import jax.numpy as jnp
from jax import lax
from jax.experimental import pallas as pl
from jax.experimental.pallas import tpu as pltpu
from jax.sharding import PartitionSpec as P

LEAF = 256
R = 64
VEC = 32
LEAF_DEV = 16
NB = 6
K_FAR = 24
NDEV = 128
GX = 8
GY = 16
F32 = jnp.float32
BF16 = jnp.bfloat16
NT = (((1,), (1,)), ((), ()))
NN = (((1,), (0,)), ((), ()))
MESH = pl.DeviceIdType.MESH
PITCH = 256


def flip(value, bits):
    for k in range(3):
        bit = 1 << k
        if bits & bit:
            value = value + bit - 2 * bit * ((value // bit) % 2)
    return value


def dot(lhs, rhs, dims):
    return lax.dot_general(lhs, rhs, dims, preferred_element_type=F32)


def swap(block):
    return jnp.concatenate([block[:, R:], block[:, :R]], axis=1)


def low_lanes(rows):
    return lax.broadcasted_iota(jnp.int32, (rows, 2 * R), 1) < R


def split(block):
    high = block.astype(BF16)
    low = (block - high.astype(F32)).astype(BF16)
    return jnp.concatenate([high, low], axis=0)


def apply(block, pair):
    both = dot(split(block), jnp.concatenate([pair, pair], axis=0), NT)
    return both[:VEC] + both[VEC:]


def apply_transposed(block, pair):
    both = dot(split(block)[:, :R], pair, NN)
    both = both[:VEC] + both[VEC:]
    return both + swap(both)


def select_heap(top, lanes, found):
    row = lax.broadcasted_iota(jnp.int32, (16, 2 * NDEV), 0)
    lane = lax.broadcasted_iota(jnp.int32, (16, 2 * NDEV), 1)
    hot = jnp.zeros((16, 2 * NDEV), F32)
    for n, index in enumerate(lanes):
        hot = jnp.where((row == n) & (lane == index), 1.0, hot)
    hot = hot.astype(BF16)

    def one(r, _):
        picked = dot(hot, split(top[r]), NT)
        found[pl.ds(r, 16, stride=R), :] = picked
        return 0

    lax.fori_loop(0, R, one, 0, unroll=8)


def matrix(found, n):
    return found[n * R : (n + 1) * R, :].astype(BF16)


def kernel(
    vec_h, tiles_h, near_s, basis_h, lt_h, far_h, far_s, tt_h, tc_h, out,
    vec, tiles, basis, lt, far, tt, tc, xe, mp, me, found_t, found_c, trees, got, box,
    lsem, ssem, rsem,
):
    a = lax.axis_index("gx")
    b = lax.axis_index("gy")
    d = a * GY + b

    def local(n, source, target):
        return pltpu.make_async_copy(source, target, lsem.at[n])

    c_vec = local(0, vec_h, vec)
    c_basis = local(1, basis_h, basis)
    c_lt = local(2, lt_h, lt)
    c_tt = local(3, tt_h, tt)
    c_tc = local(4, tc_h, tc)
    c_tiles = [local(5 + n, tiles_h.at[pl.ds(4 * n, 4)], tiles.at[pl.ds(4 * n, 4)]) for n in range(4)]
    c_far = [local(9 + n, far_h.at[pl.ds(8 * n, 8)], far.at[pl.ds(8 * n, 8)]) for n in range(2)]
    for copy in [c_vec, c_basis, c_lt, c_tt, c_tc] + c_tiles + c_far:
        copy.start()

    gx_up = ((a + 1) % GX, b)
    gx_down = ((a + GX - 1) % GX, b)
    gy_up = (a, (b + 1) % GY)
    gy_down = (a, (b + GY - 1) % GY)
    x_of = b // 4
    z_of = b % 4
    group_a = [(a, x_of * 4 + flip(z_of, i)) for i in range(1, 4)]
    group_b = [(a, flip(x_of, i) * 4 + z_of) for i in range(1, 4)]
    group_c = [(flip(a, i), b) for i in range(1, 8)]
    partners = [gx_up, gx_down, gy_up, gy_down] + group_a + group_b + group_c
    barrier = pltpu.get_barrier_semaphore()
    for partner in partners:
        pl.semaphore_signal(barrier, inc=1, device_id=partner, device_id_type=MESH)

    def remote(n, source, target, partner):
        return pltpu.make_async_remote_copy(
            src_ref=source, dst_ref=target, send_sem=ssem.at[n], recv_sem=rsem.at[n],
            device_id=partner, device_id_type=MESH,
        )

    def leaves(start, count):
        return xe.at[pl.ds(start, count)]

    x_gy = []
    for n, x in enumerate((16, 32)):
        x_gy.append(remote(2 * n, leaves(x + 8, 4), leaves(x, 4), gy_up))
        x_gy.append(remote(2 * n + 1, leaves(x + 4, 4), leaves(x + 12, 4), gy_down))
    x_gx = [
        remote(4, leaves(36, 8), leaves(4, 8), gx_up),
        remote(5, leaves(20, 8), leaves(52, 8), gx_down),
    ]
    x_corner = []
    for n, y in enumerate((0, 12)):
        x_corner.append(remote(6 + 2 * n, leaves(32 + y, 4), leaves(y, 4), gx_up))
        x_corner.append(remote(7 + 2 * n, leaves(16 + y, 4), leaves(48 + y, 4), gx_down))
    m_gy = [remote(10, mp.at[4], mp.at[3], gy_up), remote(11, mp.at[4], mp.at[5], gy_down)]
    m_gx = [remote(12, mp.at[4], mp.at[1], gx_up), remote(13, mp.at[4], mp.at[7], gx_down)]
    m_corner = [
        remote(14, mp.at[3], mp.at[0], gx_up),
        remote(15, mp.at[3], mp.at[6], gx_down),
        remote(16, mp.at[5], mp.at[2], gx_up),
        remote(17, mp.at[5], mp.at[8], gx_down),
    ]
    t_a = [remote(17 + i, trees.at[0], got.at[i], group_a[i - 1]) for i in range(1, 4)]
    t_b = [remote(20 + i, trees.at[1], got.at[4 + i], group_b[i - 1]) for i in range(1, 4)]
    t_c = [remote(23 + i, trees.at[2], got.at[8 + i], group_c[i - 1]) for i in range(1, 8)]

    c_vec.wait()
    for m in range(LEAF_DEV):
        slot = (m % 2 + 1) * 16 + (m // 2 % 2 + 1) * 4 + m // 4
        xe[slot] = vec[:, m * LEAF : (m + 1) * LEAF]
    pl.semaphore_wait(barrier, len(partners))
    for copy in x_gy + x_gx:
        copy.start()

    low = low_lanes(VEC)
    c_basis.wait()
    for q in range(LEAF_DEV // 2):
        pair = jnp.concatenate(
            [vec[:, 2 * q * LEAF : (2 * q + 1) * LEAF], vec[:, (2 * q + 1) * LEAF : (2 * q + 2) * LEAF]], axis=0
        )
        weights = jnp.concatenate([basis[2 * q], basis[2 * q + 1]], axis=0)
        both = dot(pair, weights, NT)
        mp[4, q] = jnp.where(low, both[:VEC], both[VEC:]).astype(BF16)
    for copy in m_gy + m_gx:
        copy.start()

    c_lt.wait()
    box_0 = None
    for q in range(LEAF_DEV // 2):
        weights = jnp.concatenate([lt[2 * q], lt[2 * q + 1]], axis=1)
        term = dot(mp[4, q], jnp.concatenate([weights, weights], axis=0), NT)
        box_0 = term if box_0 is None else box_0 + term

    group = [d // 2**t for t in range(7)]

    def heap(t, g):
        return (NDEV >> t) + g

    c_tt.wait()
    select_heap(
        tt,
        [
            heap(0, group[0]), heap(1, group[1]), heap(1, flip(group[1], 1)), heap(2, group[2]), heap(3, group[3]),
            heap(3, flip(group[3], 1)), heap(4, group[4]), heap(5, group[5]), heap(5, flip(group[5], 2)),
            heap(5, flip(group[5], 3)),
        ],
        found_t,
    )
    trees[0] = jnp.where(low, box_0, apply(box_0, matrix(found_t, 0)))
    for copy in t_a:
        copy.start()
    c_tc.wait()
    select_heap(tc, [heap(t, group[t]) for t in range(7)], found_c)

    for copy in x_gy:
        copy.wait_recv()
    for copy in x_corner:
        copy.start()
    for copy in m_gy:
        copy.wait_recv()
    for copy in m_corner:
        copy.start()

    def first_of(block):
        return jnp.where(low, block, swap(block))

    def second_of(block):
        return jnp.where(low, swap(block), block)

    def climb(stage, copies, own_t, sibling_t):
        for copy in copies:
            copy.wait_recv()
        base = 4 * stage
        sibling = first_of(got[base + 1])
        own = second_of(trees[stage] + got[base + 1])
        other = second_of(got[base + 2] + got[base + 3])
        above = apply(own, matrix(found_t, own_t)) + apply(other, matrix(found_t, sibling_t))
        return sibling, other, above

    sib_0, sib_1, box_2 = climb(0, t_a, 1, 2)
    trees[1] = jnp.where(low, box_2, apply(box_2, matrix(found_t, 3)))
    for copy in t_b:
        copy.start()
    box[0] = apply(sib_0, matrix(found_c, 0))
    box[1] = apply(sib_1, matrix(found_c, 1))

    for copy in x_gx + x_corner:
        copy.wait_recv()

    x_base = 20 - 32 * a - 8 * b

    def near(l, _):
        total = None
        for j in range(NB):
            index = near_s[j, l]
            slot = 63 & (
                (index >> 8) * 32 + (index & 1) * 16 + ((index >> 4) & 15) * 8
                + (index & 2) * 2 + ((index >> 2) & 3) + x_base
            )
            term = dot(xe[slot], tiles[l, j], NT)
            total = term if total is None else total + term
        out[:, pl.ds(pl.multiple_of(l * LEAF, LEAF), LEAF)] = total
        return 0

    c_tiles[0].wait()
    c_tiles[1].wait()
    lax.fori_loop(0, 8, near, 0, unroll=4)

    sib_2, sib_3, box_4 = climb(1, t_b, 4, 5)
    trees[2] = jnp.where(low, box_4, apply(box_4, matrix(found_t, 6)))
    for copy in t_c:
        copy.start()
    box[2] = apply(sib_2, matrix(found_c, 2))
    box[3] = apply(sib_3, matrix(found_c, 3))

    c_tiles[2].wait()
    c_tiles[3].wait()
    lax.fori_loop(8, 16, near, 0, unroll=4)

    for copy in m_gx + m_corner:
        copy.wait_recv()

    def unpack(p, _):
        base = (p // 3) * PITCH + (p % 3) * LEAF_DEV
        for q in range(LEAF_DEV // 2):
            pair = mp[p, q]
            other = swap(pair)
            me[base + 2 * q] = jnp.where(low, pair, other)
            me[base + 2 * q + 1] = jnp.where(low, other, pair)
        return 0

    lax.fori_loop(0, 9, unpack, 0)

    for copy in t_c:
        copy.wait_recv()
    sib_4 = first_of(got[9])
    sib_5 = second_of(got[10] + got[11])
    sib_6 = apply(second_of(got[12] + got[13]), matrix(found_t, 8)) + apply(
        second_of(got[14] + got[15]), matrix(found_t, 9)
    )
    down = apply(sib_6, matrix(found_c, 6))
    down = apply(sib_5, matrix(found_c, 5)) + apply_transposed(down, matrix(found_t, 7))
    down = apply(sib_4, matrix(found_c, 4)) + apply_transposed(down, matrix(found_t, 6))
    down = box[3] + apply_transposed(down, matrix(found_t, 4))
    down = box[2] + apply_transposed(down, matrix(found_t, 3))
    down = box[1] + apply_transposed(down, matrix(found_t, 1))
    down = box[0] + apply_transposed(down, matrix(found_t, 0))
    local_box = split(down)[:, :R]

    for copy in c_far:
        copy.wait()
    m_base = (a - 1) * PITCH + (b - 1) * LEAF_DEV

    def finish(l, _):
        total = None
        for k in range(0, K_FAR, 4):
            moment = [me[(far_s[l, k + i] - m_base) & 1023] for i in range(4)]
            left = jnp.concatenate(
                [jnp.where(low, moment[0], moment[1]), jnp.where(low, moment[2], moment[3])], axis=1
            )
            right = jnp.concatenate([far[l, k + i] for i in range(4)], axis=1)
            term = dot(left, right, NT)
            total = term if total is None else total + term
        both = dot(local_box, lt[l], NN)
        coeffs = (total + (both[:VEC] + both[VEC:])).astype(BF16)
        at = pl.ds(pl.multiple_of(l * LEAF, LEAF), LEAF)
        out[:, at] = out[:, at] + dot(coeffs, basis[l], NN)
        return 0

    lax.fori_loop(0, LEAF_DEV, finish, 0, unroll=2)

    for copy in x_gy + x_gx + x_corner + m_gy + m_gx + m_corner + t_a + t_b + t_c:
        copy.wait_send()


def per_device(
    vectors, near_tiles, near_list, leaf_basis, leaf_transfer, far_coupling, far_list, top_transfer, top_coupling
):
    any_spec = pl.BlockSpec(memory_space=pl.ANY)
    smem = pl.BlockSpec(memory_space=pltpu.SMEM)
    return pl.pallas_call(
        kernel,
        out_shape=jax.ShapeDtypeStruct((VEC, LEAF_DEV * LEAF), F32),
        in_specs=[any_spec, any_spec, smem, any_spec, any_spec, any_spec, smem, any_spec, any_spec],
        out_specs=pl.BlockSpec(memory_space=pltpu.VMEM),
        scratch_shapes=[
            pltpu.VMEM((VEC, LEAF_DEV * LEAF), BF16),
            pltpu.VMEM((LEAF_DEV, NB, LEAF, LEAF), BF16),
            pltpu.VMEM((LEAF_DEV, R, LEAF), BF16),
            pltpu.VMEM((LEAF_DEV, R, R), BF16),
            pltpu.VMEM((LEAF_DEV, K_FAR, R, R), BF16),
            pltpu.VMEM((R, R, 2 * NDEV), F32),
            pltpu.VMEM((R, R, 2 * NDEV), F32),
            pltpu.VMEM((64, VEC, LEAF), BF16),
            pltpu.VMEM((9, LEAF_DEV // 2, VEC, 2 * R), BF16),
            pltpu.VMEM((1024, VEC, 2 * R), BF16),
            pltpu.VMEM((16 * R, 2 * R), F32),
            pltpu.VMEM((16 * R, 2 * R), F32),
            pltpu.VMEM((3, VEC, 2 * R), F32),
            pltpu.VMEM((16, VEC, 2 * R), F32),
            pltpu.VMEM((4, VEC, 2 * R), F32),
            pltpu.SemaphoreType.DMA((11,)),
            pltpu.SemaphoreType.DMA((31,)),
            pltpu.SemaphoreType.DMA((31,)),
        ],
        compiler_params=pltpu.CompilerParams(
            collective_id=0, has_side_effects=True, vmem_limit_bytes=56 << 20
        ),
        cost_estimate=pl.CostEstimate(flops=600_000_000, bytes_accessed=29_000_000, transcendentals=0),
    )(
        vectors,
        near_tiles,
        near_list.T,
        leaf_basis,
        leaf_transfer,
        far_coupling,
        far_list,
        jnp.transpose(top_transfer, (1, 2, 0)),
        jnp.transpose(top_coupling, (1, 2, 0)),
    )


def solution(mesh):
    placed = (
        P(None, ("gx", "gy")),
        P(("gx", "gy"), None, None, None),
        P(("gx", "gy"), None),
        P(("gx", "gy"), None, None),
        P(("gx", "gy"), None, None),
        P(("gx", "gy"), None, None, None),
        P(("gx", "gy"), None),
        P(),
        P(),
    )
    return jax.shard_map(
        per_device, mesh=mesh, in_specs=placed, out_specs=P(None, ("gx", "gy")), check_vma=False
    )
```

```python
import jax
import jax.numpy as jnp
from jax import lax
from jax.experimental import pallas as pl
from jax.experimental.pallas import tpu as pltpu
from jax.sharding import PartitionSpec as P

LEAF = 256
R = 64
VEC = 32
LEAF_DEV = 16
NB = 6
K_FAR = 24
NDEV = 128
GX = 8
GY = 16
F32 = jnp.float32
BF16 = jnp.bfloat16
NT = (((1,), (1,)), ((), ()))
NN = (((1,), (0,)), ((), ()))
MESH = pl.DeviceIdType.MESH
PITCH = 256
PAIRS = LEAF_DEV // 2
HALF = VEC // 2


def flip(value, bits):
    for k in range(4):
        bit = 1 << k
        if bits & bit:
            value = value + bit - 2 * bit * ((value // bit) % 2)
    return value


def dot(lhs, rhs, dims):
    return lax.dot_general(lhs, rhs, dims, preferred_element_type=F32)


def swap(block):
    return jnp.concatenate([block[:, R:], block[:, :R]], axis=1)


def low_lanes(rows):
    return lax.broadcasted_iota(jnp.int32, (rows, 2 * R), 1) < R


def split(block):
    high = block.astype(BF16)
    low = (block - high.astype(F32)).astype(BF16)
    return jnp.concatenate([high, low], axis=0)


def apply(blocks, pairs):
    left = jnp.concatenate([split(block) for block in blocks], axis=1)
    right = jnp.concatenate([jnp.concatenate([pair, pair], axis=0) for pair in pairs], axis=1)
    both = dot(left, right, NT)
    rows = both.shape[0] // 2
    return both[:rows] + both[rows:]


def pair_of(block):
    high = block.astype(BF16)
    return jnp.where(low_lanes(R), high, (block - high.astype(F32)).astype(BF16))


def select_heap(top, lanes, found, rows):
    row = lax.broadcasted_iota(jnp.int32, (rows, 2 * NDEV), 0)
    lane = lax.broadcasted_iota(jnp.int32, (rows, 2 * NDEV), 1)
    wanted = jnp.full((rows, 2 * NDEV), -1, jnp.int32)
    for n, index in enumerate(lanes):
        wanted = jnp.where(row == n, index, wanted)
    hot = jnp.where(lane == wanted, 1.0, 0.0).astype(BF16)

    def one(r, _):
        found[pl.ds(r, rows, stride=R), :] = dot(hot, split(top[r]), NT)
        return 0

    lax.fori_loop(0, R, one, 0, unroll=16)


def matrix(found, n):
    return found[n * R : (n + 1) * R, :].astype(BF16)


def turned(found, n):
    block = found[n * R : (n + 1) * R, :].T
    return jnp.concatenate([block[:R], block[R:]], axis=1).astype(BF16)


def turned_whole(found, n):
    block = found[n * R : (n + 1) * R, :].T
    block = block[:R] + block[R:]
    return jnp.concatenate([block, block], axis=1)


def packed(block):
    return jnp.where(low_lanes(HALF), block[:HALF], block[HALF:])


def unpacked(block):
    low = low_lanes(HALF)
    other = swap(block)
    return jnp.concatenate([jnp.where(low, block, other), jnp.where(low, other, block)], axis=0)


def kernel(
    vec_h, tiles_h, near_s, basis_h, lt_h, far_h, far_s, tt_h, tc_h, out,
    vec, tiles, basis, lt, far, tt, tc, xe, mp, me, found_t, found_c, mine, got, got_top, near_sum, far_sum, tops,
    lsem, ssem, rsem,
):
    a = lax.axis_index("gx")
    b = lax.axis_index("gy")
    d = a * GY + b

    def local(n, source, target):
        return pltpu.make_async_copy(source, target, lsem.at[n])

    c_vec = local(0, vec_h, vec)
    c_basis = local(1, basis_h, basis)
    c_lt = local(2, lt_h, lt)
    c_tt = local(3, tt_h, tt)
    c_tc = local(4, tc_h, tc)
    c_own = local(5, tiles_h.at[:, pl.ds(0, 1)], tiles.at[:, pl.ds(0, 1)])
    c_far = local(6, far_h, far)
    c_tiles = local(7, tiles_h.at[:, pl.ds(1, NB - 1)], tiles.at[:, pl.ds(1, NB - 1)])
    ALL = [c_vec, c_basis, c_lt, c_tt, c_tc, c_own, c_far, c_tiles]
    for copy in ALL[:3]:
        copy.start()

    gx_up = ((a + 1) % GX, b)
    gx_down = ((a + GX - 1) % GX, b)
    gy_up = (a, (b + 1) % GY)
    gy_down = (a, (b + GY - 1) % GY)
    group_y = [(a, flip(b, i)) for i in range(1, GY)]
    group_x = [(flip(a, i), b) for i in range(1, GX)]
    barrier = pltpu.get_barrier_semaphore()
    for partner in group_y + group_x:
        pl.semaphore_signal(barrier, inc=1, device_id=partner, device_id_type=MESH)

    def remote(n, source, target, partner):
        return pltpu.make_async_remote_copy(
            src_ref=source, dst_ref=target, send_sem=ssem.at[n], recv_sem=rsem.at[n],
            device_id=partner, device_id_type=MESH,
        )

    def leaves(start, count):
        return xe.at[pl.ds(start, count)]

    x_gy = []
    for n, x in enumerate((16, 32)):
        x_gy.append(remote(2 * n, leaves(x + 8, 4), leaves(x, 4), gy_up))
        x_gy.append(remote(2 * n + 1, leaves(x + 4, 4), leaves(x + 12, 4), gy_down))
    x_gx = [
        remote(4, leaves(36, 8), leaves(4, 8), gx_up),
        remote(5, leaves(20, 8), leaves(52, 8), gx_down),
    ]
    x_corner = []
    for n, y in enumerate((0, 12)):
        x_corner.append(remote(6 + 2 * n, leaves(32 + y, 4), leaves(y, 4), gx_up))
        x_corner.append(remote(7 + 2 * n, leaves(16 + y, 4), leaves(48 + y, 4), gx_down))
    m_gy = [remote(10, mp.at[4], mp.at[3], gy_up), remote(11, mp.at[4], mp.at[5], gy_down)]
    m_gx = [remote(12, mp.at[4], mp.at[1], gx_up), remote(13, mp.at[4], mp.at[7], gx_down)]
    m_corner = [
        remote(14, mp.at[3], mp.at[0], gx_up),
        remote(15, mp.at[3], mp.at[6], gx_down),
        remote(16, mp.at[5], mp.at[2], gx_up),
        remote(17, mp.at[5], mp.at[8], gx_down),
    ]
    t_low = [remote(17 + i, mine.at[0], got.at[i], group_y[i - 1]) for i in range(1, GY)]
    t_top = [remote(32 + i, mine.at[1 if i == 1 else 2], got_top.at[i], group_x[i - 1]) for i in range(1, GX)]

    low = low_lanes(VEC)
    c_vec.wait()
    for m in range(LEAF_DEV):
        slot = (m % 2 + 1) * 16 + (m // 2 % 2 + 1) * 4 + m // 4
        xe[slot] = vec[:, m * LEAF : (m + 1) * LEAF]
    pl.semaphore_wait(barrier, len(group_y) + len(group_x))
    for copy in x_gy + x_gx:
        copy.start()
    c_basis.wait()
    c_lt.wait()
    for copy in ALL[3:]:
        copy.start()
    for q in range(PAIRS):
        pair = jnp.concatenate(
            [vec[:, 2 * q * LEAF : (2 * q + 1) * LEAF], vec[:, (2 * q + 1) * LEAF : (2 * q + 2) * LEAF]], axis=0
        )
        weights = jnp.concatenate([basis[2 * q], basis[2 * q + 1]], axis=0)
        both = dot(pair, weights, NT)
        mp[4, q] = jnp.where(low, both[:VEC], both[VEC:]).astype(BF16)
    box_0 = None
    for q in range(PAIRS):
        weights = jnp.concatenate([lt[2 * q], lt[2 * q + 1]], axis=1)
        term = dot(mp[4, q], jnp.concatenate([weights, weights], axis=0), NT)
        box_0 = term if box_0 is None else box_0 + term
    mine[0] = packed(box_0)
    for copy in t_low + m_gy + m_gx:
        copy.start()

    group = [d // 2**t for t in range(7)]

    def heap(t, flipped=0):
        return (NDEV >> t) + flip(group[t], flipped)

    lanes = [heap(0, i) for i in range(16)] + [heap(1, i) for i in range(8)] + [heap(2, i) for i in range(4)]
    lanes += [heap(3), heap(3, 1), heap(4), heap(5), heap(5, 2), heap(5, 3)]
    first = {0: 0, 1: 16, 2: 24, 3: 28, 4: 30, 5: 31}
    c_tt.wait()
    select_heap(tt, lanes, found_t, 48)
    c_tc.wait()
    select_heap(tc, [heap(t) for t in range(7)], found_c, 16)

    def unpack(p):
        base = (p // 3) * PITCH + (p % 3) * LEAF_DEV
        for q in range(PAIRS):
            pair = mp[p, q]
            other = swap(pair)
            me[base + 2 * q] = jnp.where(low, pair, other)
            me[base + 2 * q + 1] = jnp.where(low, other, pair)

    for copy in x_gy:
        copy.wait_recv()
    for copy in x_corner:
        copy.start()
    for copy in m_gy:
        copy.wait_recv()
    for copy in m_corner:
        copy.start()
    unpack(4)
    c_own.wait()
    for m in range(LEAF_DEV):
        near_sum[m] = dot(vec[:, m * LEAF : (m + 1) * LEAF], tiles[m, 0], NT)

    for copy in t_low:
        copy.wait_recv()
    boxes = [box_0] + [unpacked(got[i]) for i in range(1, GY)]
    siblings = []
    for t in range(4):
        siblings.append(boxes[1])
        boxes = [
            apply(
                [boxes[2 * j], boxes[2 * j + 1]],
                [matrix(found_t, first[t] + 2 * j), matrix(found_t, first[t] + 2 * j + 1)],
            )
            for j in range(len(boxes) // 2)
        ]
    mine[1] = packed(boxes[0])
    mine[2] = packed(apply(boxes, [matrix(found_t, first[4])]))
    for copy in t_top:
        copy.start()
    down = apply([siblings[3]], [matrix(found_c, 3)])
    for t in (2, 1, 0):
        down = apply([siblings[t], down], [matrix(found_c, t), turned(found_t, first[t])])

    chain = turned_whole(found_t, first[0])
    for t in (1, 2, 3):
        chain = apply([chain], [matrix(found_t, first[t])])
    top_weights = [pair_of(apply([chain], [turned(found_c, 4)]))]
    chain = apply([chain], [matrix(found_t, first[4])])
    top_weights.append(pair_of(apply([chain], [turned(found_c, 5)])))
    chain = apply([chain], [matrix(found_t, first[5])])
    chain = apply([chain], [turned(found_c, 6)])
    for n in (1, 2):
        top_weights.append(pair_of(apply([chain], [turned(found_t, first[5] + n)])))
    for n in range(4):
        tops[n] = top_weights[n]

    unpack(3)
    unpack(5)
    for copy in m_gx:
        copy.wait_recv()
    unpack(1)
    unpack(7)
    for copy in x_gx + x_corner:
        copy.wait_recv()
    c_tiles.wait()
    x_base = 20 - 32 * a - 8 * b

    def near_leaf(l, _):
        total = near_sum[l]
        for j in range(1, NB):
            index = near_s[j, l]
            slot = 63 & (
                (index >> 8) * 32 + (index & 1) * 16 + ((index >> 4) & 15) * 8
                + (index & 2) * 2 + ((index >> 2) & 3) + x_base
            )
            total = total + dot(xe[slot], tiles[l, j], NT)
        near_sum[l] = total
        return 0

    lax.fori_loop(0, LEAF_DEV, near_leaf, 0, unroll=16)

    for copy in m_corner:
        copy.wait_recv()
    for p in (0, 2, 6, 8):
        unpack(p)
    c_far.wait()
    m_base = (a - 1) * PITCH + (b - 1) * LEAF_DEV

    def far_leaf(l, _):
        total = None
        for k in range(0, K_FAR, 4):
            moment = [me[(far_s[l, k + i] - m_base) & 1023] for i in range(4)]
            left = jnp.concatenate(
                [jnp.where(low, moment[0], moment[1]), jnp.where(low, moment[2], moment[3])], axis=1
            )
            right = jnp.concatenate([far[l, k + i] for i in range(4)], axis=1)
            term = dot(left, right, NT)
            total = term if total is None else total + term
        far_sum[l] = total
        return 0

    lax.fori_loop(0, LEAF_DEV, far_leaf, 0, unroll=8)

    for copy in t_top:
        copy.wait_recv()
    top = [None] + [unpacked(got_top[i]) for i in range(1, GX)]
    down = down + apply([top[1], top[2] + top[3], top[4] + top[5], top[6] + top[7]], [tops[n] for n in range(4)])
    high = down.astype(BF16)
    rest = (down - high.astype(F32)).astype(BF16)
    local_box = jnp.where(low, high, rest)
    for m in range(LEAF_DEV):
        from_box = dot(local_box, jnp.concatenate([lt[m], lt[m]], axis=0), NN)
        coeffs = (far_sum[m] + from_box).astype(BF16)
        out[:, m * LEAF : (m + 1) * LEAF] = near_sum[m] + dot(coeffs, basis[m], NN)

    for copy in x_gy + x_gx + x_corner + m_gy + m_gx + m_corner + t_low + t_top:
        copy.wait_send()


def per_device(
    vectors, near_tiles, near_list, leaf_basis, leaf_transfer, far_coupling, far_list, top_transfer, top_coupling
):
    any_spec = pl.BlockSpec(memory_space=pltpu.HBM)
    smem = pl.BlockSpec(memory_space=pltpu.SMEM)
    return pl.pallas_call(
        kernel,
        out_shape=pltpu.VMEM((VEC, LEAF_DEV * LEAF), F32),
        in_specs=[any_spec, any_spec, smem, any_spec, any_spec, any_spec, smem, any_spec, any_spec],
        out_specs=pl.BlockSpec(memory_space=pltpu.VMEM),
        scratch_shapes=[
            pltpu.VMEM((VEC, LEAF_DEV * LEAF), BF16),
            pltpu.VMEM((LEAF_DEV, NB, LEAF, LEAF), BF16),
            pltpu.VMEM((LEAF_DEV, R, LEAF), BF16),
            pltpu.VMEM((LEAF_DEV, R, R), BF16),
            pltpu.VMEM((LEAF_DEV, K_FAR, R, R), BF16),
            pltpu.VMEM((R, R, 2 * NDEV), F32),
            pltpu.VMEM((R, R, 2 * NDEV), F32),
            pltpu.VMEM((64, VEC, LEAF), BF16),
            pltpu.VMEM((9, PAIRS, VEC, 2 * R), BF16),
            pltpu.VMEM((1024, VEC, 2 * R), BF16),
            pltpu.VMEM((48 * R, 2 * R), F32),
            pltpu.VMEM((16 * R, 2 * R), F32),
            pltpu.VMEM((3, HALF, 2 * R), F32),
            pltpu.VMEM((GY, HALF, 2 * R), F32),
            pltpu.VMEM((GX, HALF, 2 * R), F32),
            pltpu.VMEM((LEAF_DEV, VEC, LEAF), F32),
            pltpu.VMEM((LEAF_DEV, VEC, R), F32),
            pltpu.VMEM((4, R, 2 * R), BF16),
            pltpu.SemaphoreType.DMA((8,)),
            pltpu.SemaphoreType.DMA((40,)),
            pltpu.SemaphoreType.DMA((40,)),
        ],
        compiler_params=pltpu.CompilerParams(
            collective_id=0, has_side_effects=True, vmem_limit_bytes=60 << 20
        ),
        cost_estimate=pl.CostEstimate(flops=600_000_000, bytes_accessed=29_000_000, transcendentals=0),
    )(
        vectors,
        near_tiles,
        near_list.T,
        leaf_basis,
        leaf_transfer,
        far_coupling,
        far_list,
        jnp.transpose(top_transfer, (1, 2, 0)),
        jnp.transpose(top_coupling, (1, 2, 0)),
    )


def solution(mesh):
    placed = (
        P(None, ("gx", "gy")),
        P(("gx", "gy"), None, None, None),
        P(("gx", "gy"), None),
        P(("gx", "gy"), None, None),
        P(("gx", "gy"), None, None),
        P(("gx", "gy"), None, None, None),
        P(("gx", "gy"), None),
        P(),
        P(),
    )
    return jax.shard_map(
        per_device, mesh=mesh, in_specs=placed, out_specs=P(None, ("gx", "gy")), check_vma=False
    )
```

```python
import jax
import jax.numpy as jnp
from jax import lax
from jax.experimental import pallas as pl
from jax.experimental.pallas import tpu as pltpu
from jax.sharding import PartitionSpec as P

LEAF = 256
R = 64
VEC = 32
LEAF_DEV = 16
NB = 6
K_FAR = 24
NDEV = 128
GX = 8
GY = 16
F32 = jnp.float32
BF16 = jnp.bfloat16
NT = (((1,), (1,)), ((), ()))
NN = (((1,), (0,)), ((), ()))
MESH = pl.DeviceIdType.MESH
PITCH = 256
PAIRS = LEAF_DEV // 2
HALF = VEC // 2


def flip(value, bits):
    for k in range(4):
        bit = 1 << k
        if bits & bit:
            value = value + bit - 2 * bit * ((value // bit) % 2)
    return value


def dot(lhs, rhs, dims):
    return lax.dot_general(lhs, rhs, dims, preferred_element_type=F32)


def swap(block):
    return jnp.concatenate([block[:, R:], block[:, :R]], axis=1)


def low_lanes(rows):
    return lax.broadcasted_iota(jnp.int32, (rows, 2 * R), 1) < R


def split(block):
    high = block.astype(BF16)
    low = (block - high.astype(F32)).astype(BF16)
    return jnp.concatenate([high, low], axis=0)


def apply(blocks, pairs):
    left = jnp.concatenate([split(block) for block in blocks], axis=1)
    right = jnp.concatenate([jnp.concatenate([pair, pair], axis=0) for pair in pairs], axis=1)
    both = dot(left, right, NT)
    rows = both.shape[0] // 2
    return both[:rows] + both[rows:]


def pair_of(block):
    high = block.astype(BF16)
    return jnp.where(low_lanes(R), high, (block - high.astype(F32)).astype(BF16))


def select_heap(top, lanes, found, rows):
    row = lax.broadcasted_iota(jnp.int32, (rows, 2 * NDEV), 0)
    lane = lax.broadcasted_iota(jnp.int32, (rows, 2 * NDEV), 1)
    wanted = jnp.full((rows, 2 * NDEV), -1, jnp.int32)
    for n, index in enumerate(lanes):
        wanted = jnp.where(row == n, index, wanted)
    hot = jnp.where(lane == wanted, 1.0, 0.0).astype(BF16)

    def one(r, _):
        found[pl.ds(r, rows, stride=R), :] = dot(hot, split(top[r]), NT)
        return 0

    lax.fori_loop(0, R, one, 0, unroll=16)


def matrix(found, n):
    return found[n * R : (n + 1) * R, :].astype(BF16)


def turned(found, n):
    block = found[n * R : (n + 1) * R, :].T
    return jnp.concatenate([block[:R], block[R:]], axis=1).astype(BF16)


def turned_whole(found, n):
    block = found[n * R : (n + 1) * R, :].T
    block = block[:R] + block[R:]
    return jnp.concatenate([block, block], axis=1)


def packed(block):
    return jnp.where(low_lanes(HALF), block[:HALF], block[HALF:])


def unpacked(block):
    low = low_lanes(HALF)
    other = swap(block)
    return jnp.concatenate([jnp.where(low, block, other), jnp.where(low, other, block)], axis=0)


def kernel(
    vec_h, tiles_h, near_s, basis_h, lt_h, far_h, far_s, tt_h, tc_h, out,
    vec, tiles, basis, lt, far, tt, tc, xn, xf, mp, me, found_t, found_c, mine, got, got_top, near_sum, far_sum, tops,
    lsem, ssem, rsem,
):
    a = lax.axis_index("gx")
    b = lax.axis_index("gy")
    d = a * GY + b

    def local(n, source, target):
        return pltpu.make_async_copy(source, target, lsem.at[n])

    c_vec = local(0, vec_h, vec)
    c_basis = local(1, basis_h, basis)
    c_lt = local(2, lt_h, lt)
    c_tt = local(3, tt_h, tt)
    c_tc = local(4, tc_h, tc)
    c_own = local(5, tiles_h.at[:, pl.ds(0, 1)], tiles.at[:, pl.ds(0, 1)])
    c_far = local(6, far_h, far)
    c_tiles = local(7, tiles_h.at[:, pl.ds(1, NB - 1)], tiles.at[:, pl.ds(1, NB - 1)])
    ALL = [c_vec, c_basis, c_lt, c_tt, c_tc, c_own, c_tiles, c_far]
    for copy in ALL[:3]:
        copy.start()

    gx_up = ((a + 1) % GX, b)
    gx_down = ((a + GX - 1) % GX, b)
    gy_up = (a, (b + 1) % GY)
    gy_down = (a, (b + GY - 1) % GY)
    group_y = [(a, flip(b, i)) for i in range(1, GY)]
    group_x = [(flip(a, i), b) for i in range(1, GX)]
    barrier = pltpu.get_barrier_semaphore()
    for partner in group_y + group_x:
        pl.semaphore_signal(barrier, inc=1, device_id=partner, device_id_type=MESH)

    def remote(n, source, target, partner):
        return pltpu.make_async_remote_copy(
            src_ref=source, dst_ref=target, send_sem=ssem.at[n], recv_sem=rsem.at[n],
            device_id=partner, device_id_type=MESH,
        )

    core = a % 2
    chip = (flip(a, 1), b)
    off = ((a + 2 * core + GX - 1) % GX, b)

    def move(n, ref, source, target, count, partner):
        return remote(n, ref.at[pl.ds(source, count)], ref.at[pl.ds(target, count)], partner)

    x_gy = [
        move(0, xf, 24, 16, 4, gy_up), move(1, xf, 20, 28, 4, gy_down),
        move(2, xn, 24, 16, 4, gy_up), move(3, xn, 20, 28, 4, gy_down),
    ]
    x_gx = [move(4, xf, 20, 36, 8, off), move(5, xn, 20, 36, 8, chip)]
    x_corner = [
        move(6, xf, 16, 32, 4, off), move(7, xf, 28, 44, 4, off),
        move(8, xn, 16, 32, 4, chip), move(9, xn, 28, 44, 4, chip),
    ]
    m_gy = [remote(10, mp.at[4], mp.at[3], gy_up), remote(11, mp.at[4], mp.at[5], gy_down)]
    m_gx = [remote(12, mp.at[4], mp.at[1], gx_up), remote(13, mp.at[4], mp.at[7], gx_down)]
    m_corner = [
        remote(14, mp.at[3], mp.at[0], gx_up),
        remote(15, mp.at[3], mp.at[6], gx_down),
        remote(16, mp.at[5], mp.at[2], gx_up),
        remote(17, mp.at[5], mp.at[8], gx_down),
    ]
    t_low = [remote(17 + i, mine.at[0], got.at[i], group_y[i - 1]) for i in range(1, GY)]
    t_top = [remote(32 + i, mine.at[1 if i == 1 else 2], got_top.at[i], group_x[i - 1]) for i in range(1, GX)]

    low = low_lanes(VEC)
    c_vec.wait()
    for m in range(LEAF_DEV):
        place = (m // 2 % 2 + 1) * 4 + m // 4
        beside = 1 - core if m % 2 else core
        block = vec[:, m * LEAF : (m + 1) * LEAF]
        xn[beside * 16 + place] = block
        xf[(1 - beside) * 16 + place] = block
    c_basis.wait()
    c_lt.wait()
    for copy in ALL[3:]:
        copy.start()
    for q in range(PAIRS):
        pair = jnp.concatenate(
            [vec[:, 2 * q * LEAF : (2 * q + 1) * LEAF], vec[:, (2 * q + 1) * LEAF : (2 * q + 2) * LEAF]], axis=0
        )
        weights = jnp.concatenate([basis[2 * q], basis[2 * q + 1]], axis=0)
        both = dot(pair, weights, NT)
        mp[4, q] = jnp.where(low, both[:VEC], both[VEC:]).astype(BF16)
    box_0 = None
    for q in range(PAIRS):
        weights = jnp.concatenate([lt[2 * q], lt[2 * q + 1]], axis=1)
        term = dot(mp[4, q], jnp.concatenate([weights, weights], axis=0), NT)
        box_0 = term if box_0 is None else box_0 + term
    mine[0] = packed(box_0)
    pl.semaphore_wait(barrier, len(group_y) + len(group_x))
    for copy in t_low[::-1] + x_gy + m_gy + x_gx + m_gx:
        copy.start()

    group = [d // 2**t for t in range(7)]

    def heap(t, flipped=0):
        return (NDEV >> t) + flip(group[t], flipped)

    lanes = [heap(0, i) for i in range(16)] + [heap(1, i) for i in range(8)] + [heap(2, i) for i in range(4)]
    lanes += [heap(3), heap(3, 1), heap(4), heap(5), heap(5, 2), heap(5, 3)]
    first = {0: 0, 1: 16, 2: 24, 3: 28, 4: 30, 5: 31}
    c_tt.wait()
    select_heap(tt, lanes, found_t, 48)
    c_tc.wait()
    select_heap(tc, [heap(t) for t in range(7)], found_c, 16)

    def unpack(p):
        base = (p // 3) * PITCH + (p % 3) * LEAF_DEV
        for q in range(PAIRS):
            pair = mp[p, q]
            other = swap(pair)
            me[base + 2 * q] = jnp.where(low, pair, other)
            me[base + 2 * q + 1] = jnp.where(low, other, pair)

    unpack(4)
    c_own.wait()
    for m in range(LEAF_DEV):
        near_sum[m] = dot(vec[:, m * LEAF : (m + 1) * LEAF], tiles[m, 0], NT)

    chain = turned_whole(found_t, first[0])
    for t in (1, 2, 3):
        chain = apply([chain], [matrix(found_t, first[t])])
    top_weights = [pair_of(apply([chain], [turned(found_c, 4)]))]
    chain = apply([chain], [matrix(found_t, first[4])])
    top_weights.append(pair_of(apply([chain], [turned(found_c, 5)])))
    chain = apply([chain], [matrix(found_t, first[5])])
    chain = apply([chain], [turned(found_c, 6)])
    for n in (1, 2):
        top_weights.append(pair_of(apply([chain], [turned(found_t, first[5] + n)])))
    for n in range(4):
        tops[n] = top_weights[n]

    for copy in x_gy:
        copy.wait_recv()
    for copy in x_corner:
        copy.start()
    for slot in (0, 12):
        for z in range(4):
            xn[slot + z] = xf[16 + slot + z]
            xf[slot + z] = xn[16 + slot + z]
    for copy in t_low:
        copy.wait_recv()
    boxes = [box_0] + [unpacked(got[i]) for i in range(1, GY)]
    siblings = []
    for t in range(4):
        siblings.append(boxes[1])
        boxes = [
            apply(
                [boxes[2 * j], boxes[2 * j + 1]],
                [matrix(found_t, first[t] + 2 * j), matrix(found_t, first[t] + 2 * j + 1)],
            )
            for j in range(len(boxes) // 2)
        ]
    mine[1] = packed(boxes[0])
    mine[2] = packed(apply(boxes, [matrix(found_t, first[4])]))
    for copy in reversed(t_top):
        copy.start()
    for copy in m_gy:
        copy.wait_recv()
    for copy in m_corner:
        copy.start()
    def near_side(ref, copies, column, turn, base):
        for copy in copies:
            copy.wait_recv()
        base = base * 16 + turn * (16 - 32 * a) + 4 - 8 * b

        def near_leaf(i, _):
            m = column + 2 * i
            total = near_sum[m]
            for j in range(1, NB):
                index = near_s[j, m]
                slot = 63 & (
                    turn * ((index >> 8) * 32 + (index & 1) * 16) + ((index >> 4) & 15) * 8
                    + (index & 2) * 2 + ((index >> 2) & 3) + base
                )
                total = total + dot(ref[slot], tiles[m, j], NT)
            near_sum[m] = total
            return 0

        lax.fori_loop(0, PAIRS, near_leaf, 0, unroll=8)

    c_tiles.wait()
    near_side(xn, [x_gx[1]] + x_corner[2:], 1 - core, 1 - 2 * core, 3 * core - 1)
    down = apply([siblings[3]], [matrix(found_c, 3)])
    for t in (2, 1, 0):
        down = apply([siblings[t], down], [matrix(found_c, t), turned(found_t, first[t])])

    unpack(3)
    unpack(5)
    for copy in m_gx:
        copy.wait_recv()
    unpack(1)
    unpack(7)
    near_side(xf, [x_gx[0]] + x_corner[:2], core, 2 * core - 1, 2 - 3 * core)

    for copy in m_corner:
        copy.wait_recv()
    for p in (0, 2, 6, 8):
        unpack(p)
    c_far.wait()
    m_base = (a - 1) * PITCH + (b - 1) * LEAF_DEV

    def far_leaf(l, _):
        total = None
        for k in range(0, K_FAR, 4):
            moment = [me[(far_s[l, k + i] - m_base) & 1023] for i in range(4)]
            left = jnp.concatenate(
                [jnp.where(low, moment[0], moment[1]), jnp.where(low, moment[2], moment[3])], axis=1
            )
            right = jnp.concatenate([far[l, k + i] for i in range(4)], axis=1)
            term = dot(left, right, NT)
            total = term if total is None else total + term
        far_sum[l] = total
        return 0

    lax.fori_loop(0, LEAF_DEV, far_leaf, 0, unroll=8)

    for copy in t_top:
        copy.wait_recv()
    top = [None] + [unpacked(got_top[i]) for i in range(1, GX)]
    down = down + apply([top[1], top[2] + top[3], top[4] + top[5], top[6] + top[7]], [tops[n] for n in range(4)])
    high = down.astype(BF16)
    rest = (down - high.astype(F32)).astype(BF16)
    local_box = jnp.where(low, high, rest)
    for m in range(LEAF_DEV):
        from_box = dot(local_box, jnp.concatenate([lt[m], lt[m]], axis=0), NN)
        coeffs = (far_sum[m] + from_box).astype(BF16)
        out[:, m * LEAF : (m + 1) * LEAF] = near_sum[m] + dot(coeffs, basis[m], NN)

    for copy in x_gy + x_gx + x_corner + m_gy + m_gx + m_corner + t_low + t_top:
        copy.wait_send()


def per_device(
    vectors, near_tiles, near_list, leaf_basis, leaf_transfer, far_coupling, far_list, top_transfer, top_coupling
):
    any_spec = pl.BlockSpec(memory_space=pltpu.HBM)
    smem = pl.BlockSpec(memory_space=pltpu.SMEM)
    return pl.pallas_call(
        kernel,
        out_shape=pltpu.VMEM((VEC, LEAF_DEV * LEAF), F32),
        in_specs=[any_spec, any_spec, smem, any_spec, any_spec, any_spec, smem, any_spec, any_spec],
        out_specs=pl.BlockSpec(memory_space=pltpu.VMEM),
        scratch_shapes=[
            pltpu.VMEM((VEC, LEAF_DEV * LEAF), BF16),
            pltpu.VMEM((LEAF_DEV, NB, LEAF, LEAF), BF16),
            pltpu.VMEM((LEAF_DEV, R, LEAF), BF16),
            pltpu.VMEM((LEAF_DEV, R, R), BF16),
            pltpu.VMEM((LEAF_DEV, K_FAR, R, R), BF16),
            pltpu.VMEM((R, R, 2 * NDEV), F32),
            pltpu.VMEM((R, R, 2 * NDEV), F32),
            pltpu.VMEM((64, VEC, LEAF), BF16),
            pltpu.VMEM((64, VEC, LEAF), BF16),
            pltpu.VMEM((9, PAIRS, VEC, 2 * R), BF16),
            pltpu.VMEM((1024, VEC, 2 * R), BF16),
            pltpu.VMEM((48 * R, 2 * R), F32),
            pltpu.VMEM((16 * R, 2 * R), F32),
            pltpu.VMEM((3, HALF, 2 * R), F32),
            pltpu.VMEM((GY, HALF, 2 * R), F32),
            pltpu.VMEM((GX, HALF, 2 * R), F32),
            pltpu.VMEM((LEAF_DEV, VEC, LEAF), F32),
            pltpu.VMEM((LEAF_DEV, VEC, R), F32),
            pltpu.VMEM((4, R, 2 * R), BF16),
            pltpu.SemaphoreType.DMA((8,)),
            pltpu.SemaphoreType.DMA((40,)),
            pltpu.SemaphoreType.DMA((40,)),
        ],
        compiler_params=pltpu.CompilerParams(
            collective_id=0, has_side_effects=True, vmem_limit_bytes=60 << 20
        ),
        cost_estimate=pl.CostEstimate(flops=600_000_000, bytes_accessed=29_000_000, transcendentals=0),
    )(
        vectors,
        near_tiles,
        near_list.T,
        leaf_basis,
        leaf_transfer,
        far_coupling,
        far_list,
        jnp.transpose(top_transfer, (1, 2, 0)),
        jnp.transpose(top_coupling, (1, 2, 0)),
    )


def solution(mesh):
    placed = (
        P(None, ("gx", "gy")),
        P(("gx", "gy"), None, None, None),
        P(("gx", "gy"), None),
        P(("gx", "gy"), None, None),
        P(("gx", "gy"), None, None),
        P(("gx", "gy"), None, None, None),
        P(("gx", "gy"), None),
        P(),
        P(),
    )
    return jax.shard_map(
        per_device, mesh=mesh, in_specs=placed, out_specs=P(None, ("gx", "gy")), check_vma=False
    )
```

```python
import jax
import jax.numpy as jnp
from jax import lax
from jax.experimental import pallas as pl
from jax.experimental.pallas import tpu as pltpu
from jax.sharding import PartitionSpec as P

LEAF = 256
R = 64
VEC = 32
LEAF_DEV = 16
NB = 6
K_FAR = 24
NDEV = 128
GX = 8
GY = 16
F32 = jnp.float32
BF16 = jnp.bfloat16
NT = (((1,), (1,)), ((), ()))
NN = (((1,), (0,)), ((), ()))
MESH = pl.DeviceIdType.MESH
PITCH = 256
PAIRS = LEAF_DEV // 2
HALF = VEC // 2


def flip(value, bits):
    for k in range(4):
        bit = 1 << k
        if bits & bit:
            value = value + bit - 2 * bit * ((value // bit) % 2)
    return value


def dot(lhs, rhs, dims):
    return lax.dot_general(lhs, rhs, dims, preferred_element_type=F32)


def swap(block):
    return jnp.concatenate([block[:, R:], block[:, :R]], axis=1)


def low_lanes(rows):
    return lax.broadcasted_iota(jnp.int32, (rows, 2 * R), 1) < R


def split(block):
    high = block.astype(BF16)
    low = (block - high.astype(F32)).astype(BF16)
    return jnp.concatenate([high, low], axis=0)


def apply(blocks, pairs):
    left = jnp.concatenate([split(block) for block in blocks], axis=1)
    right = jnp.concatenate([jnp.concatenate([pair, pair], axis=0) for pair in pairs], axis=1)
    both = dot(left, right, NT)
    rows = both.shape[0] // 2
    return both[:rows] + both[rows:]


def pair_of(block):
    high = block.astype(BF16)
    return jnp.where(low_lanes(R), high, (block - high.astype(F32)).astype(BF16))


def select_heap(top, lanes, found, rows):
    row = lax.broadcasted_iota(jnp.int32, (rows, 2 * NDEV), 0)
    lane = lax.broadcasted_iota(jnp.int32, (rows, 2 * NDEV), 1)
    wanted = jnp.full((rows, 2 * NDEV), -1, jnp.int32)
    for n, index in enumerate(lanes):
        wanted = jnp.where(row == n, index, wanted)
    hot = jnp.where(lane == wanted, 1.0, 0.0).astype(BF16)

    def one(r, _):
        found[pl.ds(r, rows, stride=R), :] = dot(hot, split(top[r]), NT)
        return 0

    lax.fori_loop(0, R, one, 0, unroll=16)


def matrix(found, n):
    return found[n * R : (n + 1) * R, :].astype(BF16)


def turned(found, n):
    block = found[n * R : (n + 1) * R, :].T
    return jnp.concatenate([block[:R], block[R:]], axis=1).astype(BF16)


def turned_whole(found, n):
    block = found[n * R : (n + 1) * R, :].T
    block = block[:R] + block[R:]
    return jnp.concatenate([block, block], axis=1)


def packed(block):
    return jnp.where(low_lanes(HALF), block[:HALF], block[HALF:])


def unpacked(block):
    low = low_lanes(HALF)
    other = swap(block)
    return jnp.concatenate([jnp.where(low, block, other), jnp.where(low, other, block)], axis=0)


def kernel(
    vec_h, tiles_h, near_h, basis_h, lt_h, far_h, list_h, tt_h, tc_h, out,
    vec, tiles, basis, lt, far, tt, tc, xn, xf, mp, me, found_t, found_c, mine, got, got_top, near_sum, far_sum, tops, near_s, far_s,
    lsem, ssem, rsem,
):
    a = lax.axis_index("gx")
    b = lax.axis_index("gy")
    d = a * GY + b

    def local(n, source, target):
        return pltpu.make_async_copy(source, target, lsem.at[n])

    c_vec = local(0, vec_h, vec)
    c_basis = local(1, basis_h, basis)
    c_lt = local(2, lt_h, lt)
    c_tt = local(3, tt_h, tt)
    c_tc = local(4, tc_h, tc)
    c_own = local(5, tiles_h.at[:, pl.ds(0, 1)], tiles.at[:, pl.ds(0, 1)])
    c_far = local(6, far_h, far)
    c_tiles = local(7, tiles_h.at[:, pl.ds(1, NB - 1)], tiles.at[:, pl.ds(1, NB - 1)])
    c_near_list = local(8, near_h, near_s)
    c_far_list = local(9, list_h, far_s)
    ALL = [c_vec, c_basis, c_lt, c_tt, c_tc, c_own, c_tiles, c_far, c_near_list, c_far_list]
    for copy in ALL[:3]:
        copy.start()

    gx_up = ((a + 1) % GX, b)
    gx_down = ((a + GX - 1) % GX, b)
    gy_up = (a, (b + 1) % GY)
    gy_down = (a, (b + GY - 1) % GY)
    group_y = [(a, flip(b, i)) for i in range(1, GY)]
    group_x = [(flip(a, i), b) for i in range(1, GX)]
    barrier = pltpu.get_barrier_semaphore()
    for partner in group_y + group_x:
        pl.semaphore_signal(barrier, inc=1, device_id=partner, device_id_type=MESH)

    def remote(n, source, target, partner):
        return pltpu.make_async_remote_copy(
            src_ref=source, dst_ref=target, send_sem=ssem.at[n], recv_sem=rsem.at[n],
            device_id=partner, device_id_type=MESH,
        )

    core = a % 2
    chip = (flip(a, 1), b)
    off = ((a + 2 * core + GX - 1) % GX, b)

    def move(n, ref, source, target, count, partner):
        return remote(n, ref.at[pl.ds(source, count)], ref.at[pl.ds(target, count)], partner)

    x_gy = [
        move(0, xf, 24, 16, 4, gy_up), move(1, xf, 20, 28, 4, gy_down),
        move(2, xn, 24, 16, 4, gy_up), move(3, xn, 20, 28, 4, gy_down),
    ]
    x_gx = [move(4, xf, 20, 36, 8, off), move(5, xn, 20, 36, 8, chip)]
    x_corner = [
        move(6, xf, 16, 32, 4, off), move(7, xf, 28, 44, 4, off),
        move(8, xn, 16, 32, 4, chip), move(9, xn, 28, 44, 4, chip),
    ]
    m_gy = [remote(10, mp.at[4], mp.at[3], gy_up), remote(11, mp.at[4], mp.at[5], gy_down)]
    m_gx = [remote(12, mp.at[4], mp.at[1], gx_up), remote(13, mp.at[4], mp.at[7], gx_down)]
    m_corner = [
        remote(14, mp.at[3], mp.at[0], gx_up),
        remote(15, mp.at[3], mp.at[6], gx_down),
        remote(16, mp.at[5], mp.at[2], gx_up),
        remote(17, mp.at[5], mp.at[8], gx_down),
    ]
    t_low = [remote(17 + i, mine.at[0], got.at[i], group_y[i - 1]) for i in range(1, GY)]
    t_top = [remote(32 + i, mine.at[1 if i == 1 else 2], got_top.at[i], group_x[i - 1]) for i in range(1, GX)]

    low = low_lanes(VEC)
    c_vec.wait()
    for m in range(LEAF_DEV):
        place = (m // 2 % 2 + 1) * 4 + m // 4
        beside = 1 - core if m % 2 else core
        block = vec[:, m * LEAF : (m + 1) * LEAF]
        xn[beside * 16 + place] = block
        xf[(1 - beside) * 16 + place] = block
    c_basis.wait()
    c_lt.wait()
    for copy in ALL[3:]:
        copy.start()
    for q in range(PAIRS):
        pair = jnp.concatenate(
            [vec[:, 2 * q * LEAF : (2 * q + 1) * LEAF], vec[:, (2 * q + 1) * LEAF : (2 * q + 2) * LEAF]], axis=0
        )
        weights = jnp.concatenate([basis[2 * q], basis[2 * q + 1]], axis=0)
        both = dot(pair, weights, NT)
        mp[4, q] = jnp.where(low, both[:VEC], both[VEC:]).astype(BF16)
    box_0 = None
    for q in range(PAIRS):
        weights = jnp.concatenate([lt[2 * q], lt[2 * q + 1]], axis=1)
        term = dot(mp[4, q], jnp.concatenate([weights, weights], axis=0), NT)
        box_0 = term if box_0 is None else box_0 + term
    mine[0] = packed(box_0)
    pl.semaphore_wait(barrier, len(group_y) + len(group_x))
    for copy in t_low[::-1] + x_gy + m_gy + x_gx + m_gx:
        copy.start()

    group = [d // 2**t for t in range(7)]

    def heap(t, flipped=0):
        return (NDEV >> t) + flip(group[t], flipped)

    lanes = [heap(0, i) for i in range(16)] + [heap(1, i) for i in range(8)] + [heap(2, i) for i in range(4)]
    lanes += [heap(3), heap(3, 1), heap(4), heap(5), heap(5, 2), heap(5, 3)]
    first = {0: 0, 1: 16, 2: 24, 3: 28, 4: 30, 5: 31}
    c_tt.wait()
    select_heap(tt, lanes, found_t, 48)
    c_tc.wait()
    select_heap(tc, [heap(t) for t in range(7)], found_c, 16)

    def unpack(p):
        base = (p // 3) * PITCH + (p % 3) * LEAF_DEV
        for q in range(PAIRS):
            pair = mp[p, q]
            other = swap(pair)
            me[base + 2 * q] = jnp.where(low, pair, other)
            me[base + 2 * q + 1] = jnp.where(low, other, pair)

    unpack(4)
    c_own.wait()
    for m in range(LEAF_DEV):
        near_sum[m] = dot(vec[:, m * LEAF : (m + 1) * LEAF], tiles[m, 0], NT)

    chain = turned_whole(found_t, first[0])
    for t in (1, 2, 3):
        chain = apply([chain], [matrix(found_t, first[t])])
    top_weights = [pair_of(apply([chain], [turned(found_c, 4)]))]
    chain = apply([chain], [matrix(found_t, first[4])])
    top_weights.append(pair_of(apply([chain], [turned(found_c, 5)])))
    chain = apply([chain], [matrix(found_t, first[5])])
    chain = apply([chain], [turned(found_c, 6)])
    for n in (1, 2):
        top_weights.append(pair_of(apply([chain], [turned(found_t, first[5] + n)])))
    for n in range(4):
        tops[n] = top_weights[n]

    for copy in x_gy:
        copy.wait_recv()
    for copy in x_corner:
        copy.start()
    for slot in (0, 12):
        for z in range(4):
            xn[slot + z] = xf[16 + slot + z]
            xf[slot + z] = xn[16 + slot + z]
    for copy in t_low:
        copy.wait_recv()
    boxes = [box_0] + [unpacked(got[i]) for i in range(1, GY)]
    siblings = []
    for t in range(4):
        siblings.append(boxes[1])
        boxes = [
            apply(
                [boxes[2 * j], boxes[2 * j + 1]],
                [matrix(found_t, first[t] + 2 * j), matrix(found_t, first[t] + 2 * j + 1)],
            )
            for j in range(len(boxes) // 2)
        ]
    mine[1] = packed(boxes[0])
    mine[2] = packed(apply(boxes, [matrix(found_t, first[4])]))
    for copy in reversed(t_top):
        copy.start()
    for copy in m_gy:
        copy.wait_recv()
    for copy in m_corner:
        copy.start()
    def near_side(ref, copies, column, turn, base):
        for copy in copies:
            copy.wait_recv()
        base = base * 16 + turn * (16 - 32 * a) + 4 - 8 * b

        def near_leaf(i, _):
            m = column + 2 * i
            total = near_sum[m]
            for j in range(1, NB):
                index = near_s[j, m]
                slot = 63 & (
                    turn * ((index >> 8) * 32 + (index & 1) * 16) + ((index >> 4) & 15) * 8
                    + (index & 2) * 2 + ((index >> 2) & 3) + base
                )
                total = total + dot(ref[slot], tiles[m, j], NT)
            near_sum[m] = total
            return 0

        lax.fori_loop(0, PAIRS, near_leaf, 0, unroll=8)

    c_tiles.wait()
    c_near_list.wait()
    c_far_list.wait()
    near_side(xn, [x_gx[1]] + x_corner[2:], 1 - core, 1 - 2 * core, 3 * core - 1)
    down = apply([siblings[3]], [matrix(found_c, 3)])
    for t in (2, 1, 0):
        down = apply([siblings[t], down], [matrix(found_c, t), turned(found_t, first[t])])

    unpack(3)
    unpack(5)
    for copy in m_gx:
        copy.wait_recv()
    unpack(1)
    unpack(7)
    for copy in x_gy + x_gx + m_gy + m_gx + t_low:
        copy.wait_send()
    near_side(xf, [x_gx[0]] + x_corner[:2], core, 2 * core - 1, 2 - 3 * core)

    for copy in m_corner:
        copy.wait_recv()
    for p in (0, 2, 6, 8):
        unpack(p)
    c_far.wait()
    m_base = (a - 1) * PITCH + (b - 1) * LEAF_DEV

    def far_leaf(l, _):
        total = None
        for k in range(0, K_FAR, 4):
            moment = [me[(far_s[l, k + i] - m_base) & 1023] for i in range(4)]
            left = jnp.concatenate(
                [jnp.where(low, moment[0], moment[1]), jnp.where(low, moment[2], moment[3])], axis=1
            )
            right = jnp.concatenate([far[l, k + i] for i in range(4)], axis=1)
            term = dot(left, right, NT)
            total = term if total is None else total + term
        far_sum[l] = total
        return 0

    lax.fori_loop(0, LEAF_DEV, far_leaf, 0, unroll=8)

    for copy in t_top:
        copy.wait_recv()
    top = [None] + [unpacked(got_top[i]) for i in range(1, GX)]
    down = down + apply([top[1], top[2] + top[3], top[4] + top[5], top[6] + top[7]], [tops[n] for n in range(4)])
    high = down.astype(BF16)
    rest = (down - high.astype(F32)).astype(BF16)
    local_box = jnp.where(low, high, rest)
    for m in range(LEAF_DEV):
        from_box = dot(local_box, jnp.concatenate([lt[m], lt[m]], axis=0), NN)
        coeffs = (far_sum[m] + from_box).astype(BF16)
        out[:, m * LEAF : (m + 1) * LEAF] = near_sum[m] + dot(coeffs, basis[m], NN)

    for copy in x_corner + m_corner + t_top:
        copy.wait_send()


def per_device(
    vectors, near_tiles, near_list, leaf_basis, leaf_transfer, far_coupling, far_list, top_transfer, top_coupling
):
    any_spec = pl.BlockSpec(memory_space=pltpu.HBM)
    return pl.pallas_call(
        kernel,
        out_shape=pltpu.VMEM((VEC, LEAF_DEV * LEAF), F32),
        in_specs=[any_spec] * 9,
        out_specs=pl.BlockSpec(memory_space=pltpu.VMEM),
        scratch_shapes=[
            pltpu.VMEM((VEC, LEAF_DEV * LEAF), BF16),
            pltpu.VMEM((LEAF_DEV, NB, LEAF, LEAF), BF16),
            pltpu.VMEM((LEAF_DEV, R, LEAF), BF16),
            pltpu.VMEM((LEAF_DEV, R, R), BF16),
            pltpu.VMEM((LEAF_DEV, K_FAR, R, R), BF16),
            pltpu.VMEM((R, R, 2 * NDEV), F32),
            pltpu.VMEM((R, R, 2 * NDEV), F32),
            pltpu.VMEM((64, VEC, LEAF), BF16),
            pltpu.VMEM((64, VEC, LEAF), BF16),
            pltpu.VMEM((9, PAIRS, VEC, 2 * R), BF16),
            pltpu.VMEM((1024, VEC, 2 * R), BF16),
            pltpu.VMEM((48 * R, 2 * R), F32),
            pltpu.VMEM((16 * R, 2 * R), F32),
            pltpu.VMEM((3, HALF, 2 * R), F32),
            pltpu.VMEM((GY, HALF, 2 * R), F32),
            pltpu.VMEM((GX, HALF, 2 * R), F32),
            pltpu.VMEM((LEAF_DEV, VEC, LEAF), F32),
            pltpu.VMEM((LEAF_DEV, VEC, R), F32),
            pltpu.VMEM((4, R, 2 * R), BF16),
            pltpu.SMEM((NB, LEAF_DEV), jnp.int32),
            pltpu.SMEM((LEAF_DEV, K_FAR), jnp.int32),
            pltpu.SemaphoreType.DMA((10,)),
            pltpu.SemaphoreType.DMA((40,)),
            pltpu.SemaphoreType.DMA((40,)),
        ],
        compiler_params=pltpu.CompilerParams(
            collective_id=0, has_side_effects=True, vmem_limit_bytes=60 << 20
        ),
        cost_estimate=pl.CostEstimate(flops=600_000_000, bytes_accessed=29_000_000, transcendentals=0),
    )(
        vectors,
        near_tiles,
        near_list.T,
        leaf_basis,
        leaf_transfer,
        far_coupling,
        far_list,
        jnp.transpose(top_transfer, (1, 2, 0)),
        jnp.transpose(top_coupling, (1, 2, 0)),
    )


def solution(mesh):
    placed = (
        P(None, ("gx", "gy")),
        P(("gx", "gy"), None, None, None),
        P(("gx", "gy"), None),
        P(("gx", "gy"), None, None),
        P(("gx", "gy"), None, None),
        P(("gx", "gy"), None, None, None),
        P(("gx", "gy"), None),
        P(),
        P(),
    )
    return jax.shard_map(
        per_device, mesh=mesh, in_specs=placed, out_specs=P(None, ("gx", "gy")), check_vma=False
    )
```

```python
import jax
import jax.numpy as jnp
from jax import lax
from jax.experimental import pallas as pl
from jax.experimental.pallas import tpu as pltpu
from jax.sharding import PartitionSpec as P

LEAF = 256
R = 64
VEC = 32
LEAF_DEV = 16
NB = 6
K_FAR = 24
NDEV = 128
GX = 8
GY = 16
F32 = jnp.float32
BF16 = jnp.bfloat16
NT = (((1,), (1,)), ((), ()))
NN = (((1,), (0,)), ((), ()))
MESH = pl.DeviceIdType.MESH
PITCH = 256
PAIRS = LEAF_DEV // 2
HALF = VEC // 2


def flip(value, bits):
    for k in range(4):
        bit = 1 << k
        if bits & bit:
            value = value + bit - 2 * bit * ((value // bit) % 2)
    return value


def dot(lhs, rhs, dims):
    return lax.dot_general(lhs, rhs, dims, preferred_element_type=F32)


def swap(block):
    return jnp.concatenate([block[:, R:], block[:, :R]], axis=1)


def low_lanes(rows):
    return lax.broadcasted_iota(jnp.int32, (rows, 2 * R), 1) < R


def split(block):
    high = block.astype(BF16)
    low = (block - high.astype(F32)).astype(BF16)
    return jnp.concatenate([high, low], axis=0)


def apply(blocks, pairs):
    left = jnp.concatenate([split(block) for block in blocks], axis=1)
    right = jnp.concatenate([jnp.concatenate([pair, pair], axis=0) for pair in pairs], axis=1)
    both = dot(left, right, NT)
    rows = both.shape[0] // 2
    return both[:rows] + both[rows:]


def pair_of(block):
    high = block.astype(BF16)
    return jnp.where(low_lanes(R), high, (block - high.astype(F32)).astype(BF16))


def select_heap(top, lanes, found, rows):
    row = lax.broadcasted_iota(jnp.int32, (rows, 2 * NDEV), 0)
    lane = lax.broadcasted_iota(jnp.int32, (rows, 2 * NDEV), 1)
    wanted = jnp.full((rows, 2 * NDEV), -1, jnp.int32)
    for n, index in enumerate(lanes):
        wanted = jnp.where(row == n, index, wanted)
    hot = jnp.where(lane == wanted, 1.0, 0.0).astype(BF16)

    def one(r, _):
        found[pl.ds(r, rows, stride=R), :] = dot(hot, split(top[r]), NT)
        return 0

    lax.fori_loop(0, R, one, 0, unroll=16)


def matrix(found, n):
    return found[n * R : (n + 1) * R, :].astype(BF16)


def turned(found, n):
    block = found[n * R : (n + 1) * R, :].T
    return jnp.concatenate([block[:R], block[R:]], axis=1).astype(BF16)


def turned_whole(found, n):
    block = found[n * R : (n + 1) * R, :].T
    block = block[:R] + block[R:]
    return jnp.concatenate([block, block], axis=1)


def packed(block):
    return jnp.where(low_lanes(HALF), block[:HALF], block[HALF:])


def unpacked(block):
    low = low_lanes(HALF)
    other = swap(block)
    return jnp.concatenate([jnp.where(low, block, other), jnp.where(low, other, block)], axis=0)


def kernel(
    vec_h, tiles_h, near_h, basis_h, lt_h, far_h, list_h, tt_h, tc_h, out,
    vec, tiles, basis, lt, far, tt, tc, xn, xf, mp, me, found_t, found_c, mine, got, got_top, near_sum, far_sum, tops, near_s, far_s,
    lsem, ssem, rsem,
):
    a = lax.axis_index("gx")
    b = lax.axis_index("gy")
    d = a * GY + b

    def local(n, source, target):
        return pltpu.make_async_copy(source, target, lsem.at[n])

    c_vec = local(0, vec_h, vec)
    c_basis = local(1, basis_h, basis)
    c_lt = local(2, lt_h, lt)
    c_tt = local(3, tt_h, tt)
    c_tc = local(4, tc_h, tc)
    c_own = local(5, tiles_h.at[:, pl.ds(0, 1)], tiles.at[:, pl.ds(0, 1)])
    c_far = local(6, far_h, far)
    c_tiles = local(7, tiles_h.at[:, pl.ds(1, NB - 1)], tiles.at[:, pl.ds(1, NB - 1)])
    c_near_list = local(8, near_h, near_s)
    c_far_list = local(9, list_h, far_s)
    ALL = [c_vec, c_basis, c_lt, c_tt, c_tc, c_own, c_tiles, c_far, c_near_list, c_far_list]

    gx_up = ((a + 1) % GX, b)
    gx_down = ((a + GX - 1) % GX, b)
    gy_up = (a, (b + 1) % GY)
    gy_down = (a, (b + GY - 1) % GY)
    group_y = [(a, flip(b, i)) for i in range(1, GY)]
    group_x = [(flip(a, i), b) for i in range(1, GX)]
    barrier = pltpu.get_barrier_semaphore()
    for partner in group_y[::-1] + group_x[::-1]:
        pl.semaphore_signal(barrier, inc=1, device_id=partner, device_id_type=MESH)
    for copy in ALL[:3]:
        copy.start()

    def remote(n, source, target, partner):
        return pltpu.make_async_remote_copy(
            src_ref=source, dst_ref=target, send_sem=ssem.at[n], recv_sem=rsem.at[n],
            device_id=partner, device_id_type=MESH,
        )

    core = a % 2
    chip = (flip(a, 1), b)
    off = ((a + 2 * core + GX - 1) % GX, b)

    def move(n, ref, source, target, count, partner):
        return remote(n, ref.at[pl.ds(source, count)], ref.at[pl.ds(target, count)], partner)

    x_gy = [
        move(0, xf, 24, 16, 4, gy_up), move(1, xf, 20, 28, 4, gy_down),
        move(2, xn, 24, 16, 4, gy_up), move(3, xn, 20, 28, 4, gy_down),
    ]
    x_gx = [move(4, xf, 20, 36, 8, off), move(5, xn, 20, 36, 8, chip)]
    x_corner = [
        move(6, xf, 16, 32, 4, off), move(7, xf, 28, 44, 4, off),
        move(8, xn, 16, 32, 4, chip), move(9, xn, 28, 44, 4, chip),
    ]
    m_gy = [remote(10, mp.at[4], mp.at[3], gy_up), remote(11, mp.at[4], mp.at[5], gy_down)]
    m_gx = [remote(12, mp.at[4], mp.at[1], gx_up), remote(13, mp.at[4], mp.at[7], gx_down)]
    m_corner = [
        remote(14, mp.at[3], mp.at[0], gx_up),
        remote(15, mp.at[3], mp.at[6], gx_down),
        remote(16, mp.at[5], mp.at[2], gx_up),
        remote(17, mp.at[5], mp.at[8], gx_down),
    ]
    t_low = [remote(17 + i, mine.at[0], got.at[i], group_y[i - 1]) for i in range(1, GY)]
    t_top = [remote(32 + i, mine.at[1 if i == 1 else 2], got_top.at[i], group_x[i - 1]) for i in range(1, GX)]

    low = low_lanes(VEC)
    c_vec.wait()
    for m in range(LEAF_DEV):
        place = (m // 2 % 2 + 1) * 4 + m // 4
        beside = 1 - core if m % 2 else core
        block = vec[:, m * LEAF : (m + 1) * LEAF]
        xn[beside * 16 + place] = block
        xf[(1 - beside) * 16 + place] = block
    c_basis.wait()
    c_lt.wait()
    for copy in ALL[3:]:
        copy.start()
    for q in range(PAIRS):
        pair = jnp.concatenate(
            [vec[:, 2 * q * LEAF : (2 * q + 1) * LEAF], vec[:, (2 * q + 1) * LEAF : (2 * q + 2) * LEAF]], axis=0
        )
        weights = jnp.concatenate([basis[2 * q], basis[2 * q + 1]], axis=0)
        both = dot(pair, weights, NT)
        mp[4, q] = jnp.where(low, both[:VEC], both[VEC:]).astype(BF16)
    box_0 = None
    for q in range(PAIRS):
        weights = jnp.concatenate([lt[2 * q], lt[2 * q + 1]], axis=1)
        term = dot(mp[4, q], jnp.concatenate([weights, weights], axis=0), NT)
        box_0 = term if box_0 is None else box_0 + term
    mine[0] = packed(box_0)
    pl.semaphore_wait(barrier, len(group_y) + len(group_x))
    for copy in t_low[::-1] + x_gy + m_gy + x_gx + m_gx:
        copy.start()

    group = [d // 2**t for t in range(7)]

    def heap(t, flipped=0):
        return (NDEV >> t) + flip(group[t], flipped)

    lanes = [heap(0, i) for i in range(16)] + [heap(1, i) for i in range(8)] + [heap(2, i) for i in range(4)]
    lanes += [heap(3), heap(3, 1), heap(4), heap(5), heap(5, 2), heap(5, 3)]
    first = {0: 0, 1: 16, 2: 24, 3: 28, 4: 30, 5: 31}
    c_tt.wait()
    select_heap(tt, lanes, found_t, 48)
    c_tc.wait()
    select_heap(tc, [heap(t) for t in range(7)], found_c, 16)

    def unpack(p):
        base = (p // 3) * PITCH + (p % 3) * LEAF_DEV
        for q in range(PAIRS):
            pair = mp[p, q]
            other = swap(pair)
            me[base + 2 * q] = jnp.where(low, pair, other)
            me[base + 2 * q + 1] = jnp.where(low, other, pair)

    unpack(4)
    c_own.wait()
    for m in range(LEAF_DEV):
        near_sum[m] = dot(vec[:, m * LEAF : (m + 1) * LEAF], tiles[m, 0], NT)

    for copy in x_gy[:2]:
        copy.wait_recv()
    for copy in x_corner[:2]:
        copy.start()
    chain = turned_whole(found_t, first[0])
    for t in (1, 2, 3):
        chain = apply([chain], [matrix(found_t, first[t])])
    top_weights = [pair_of(apply([chain], [turned(found_c, 4)]))]
    chain = apply([chain], [matrix(found_t, first[4])])
    top_weights.append(pair_of(apply([chain], [turned(found_c, 5)])))
    chain = apply([chain], [matrix(found_t, first[5])])
    chain = apply([chain], [turned(found_c, 6)])
    for n in (1, 2):
        top_weights.append(pair_of(apply([chain], [turned(found_t, first[5] + n)])))
    for n in range(4):
        tops[n] = top_weights[n]

    for copy in x_gy[2:]:
        copy.wait_recv()
    for copy in x_corner[2:]:
        copy.start()
    for slot in (0, 12):
        for z in range(4):
            xn[slot + z] = xf[16 + slot + z]
            xf[slot + z] = xn[16 + slot + z]
    for copy in t_low:
        copy.wait_recv()
    boxes = [box_0] + [unpacked(got[i]) for i in range(1, GY)]
    siblings = []
    for t in range(4):
        siblings.append(boxes[1])
        boxes = [
            apply(
                [boxes[2 * j], boxes[2 * j + 1]],
                [matrix(found_t, first[t] + 2 * j), matrix(found_t, first[t] + 2 * j + 1)],
            )
            for j in range(len(boxes) // 2)
        ]
    mine[1] = packed(boxes[0])
    mine[2] = packed(apply(boxes, [matrix(found_t, first[4])]))
    for copy in reversed(t_top):
        copy.start()
    for copy in m_gy:
        copy.wait_recv()
    for copy in m_corner:
        copy.start()
    def near_side(ref, copies, column, turn, base):
        for copy in copies:
            copy.wait_recv()
        base = base * 16 + turn * (16 - 32 * a) + 4 - 8 * b

        def near_leaf(i, _):
            m = column + 2 * i
            total = near_sum[m]
            for j in range(1, NB):
                index = near_s[j, m]
                slot = 63 & (
                    turn * ((index >> 8) * 32 + (index & 1) * 16) + ((index >> 4) & 15) * 8
                    + (index & 2) * 2 + ((index >> 2) & 3) + base
                )
                total = total + dot(ref[slot], tiles[m, j], NT)
            near_sum[m] = total
            return 0

        lax.fori_loop(0, PAIRS, near_leaf, 0, unroll=8)

    c_tiles.wait()
    c_near_list.wait()
    c_far_list.wait()
    near_side(xn, [x_gx[1]] + x_corner[2:], 1 - core, 1 - 2 * core, 3 * core - 1)
    down = apply([siblings[3]], [matrix(found_c, 3)])
    for t in (2, 1, 0):
        down = apply([siblings[t], down], [matrix(found_c, t), turned(found_t, first[t])])

    unpack(3)
    unpack(5)
    for copy in m_gx:
        copy.wait_recv()
    unpack(1)
    unpack(7)
    for copy in x_gy + x_gx + m_gy + m_gx + t_low:
        copy.wait_send()
    near_side(xf, [x_gx[0]] + x_corner[:2], core, 2 * core - 1, 2 - 3 * core)

    for copy in m_corner:
        copy.wait_recv()
    for p in (0, 2, 6, 8):
        unpack(p)
    c_far.wait()
    m_base = (a - 1) * PITCH + (b - 1) * LEAF_DEV

    def far_leaf(l, _):
        total = None
        for k in range(0, K_FAR, 4):
            moment = [me[(far_s[l, k + i] - m_base) & 1023] for i in range(4)]
            left = jnp.concatenate(
                [jnp.where(low, moment[0], moment[1]), jnp.where(low, moment[2], moment[3])], axis=1
            )
            right = jnp.concatenate([far[l, k + i] for i in range(4)], axis=1)
            term = dot(left, right, NT)
            total = term if total is None else total + term
        far_sum[l] = total
        return 0

    lax.fori_loop(0, LEAF_DEV, far_leaf, 0, unroll=8)

    for copy in t_top:
        copy.wait_recv()
    top = [None] + [unpacked(got_top[i]) for i in range(1, GX)]
    down = down + apply([top[1], top[2] + top[3], top[4] + top[5], top[6] + top[7]], [tops[n] for n in range(4)])
    high = down.astype(BF16)
    rest = (down - high.astype(F32)).astype(BF16)
    local_box = jnp.where(low, high, rest)
    for m in range(LEAF_DEV):
        from_box = dot(local_box, jnp.concatenate([lt[m], lt[m]], axis=0), NN)
        coeffs = (far_sum[m] + from_box).astype(BF16)
        out[:, m * LEAF : (m + 1) * LEAF] = near_sum[m] + dot(coeffs, basis[m], NN)

    for copy in x_corner + m_corner + t_top:
        copy.wait_send()


def per_device(
    vectors, near_tiles, near_list, leaf_basis, leaf_transfer, far_coupling, far_list, top_transfer, top_coupling
):
    any_spec = pl.BlockSpec(memory_space=pltpu.HBM)
    return pl.pallas_call(
        kernel,
        out_shape=pltpu.VMEM((VEC, LEAF_DEV * LEAF), F32),
        in_specs=[any_spec] * 9,
        out_specs=pl.BlockSpec(memory_space=pltpu.VMEM),
        scratch_shapes=[
            pltpu.VMEM((VEC, LEAF_DEV * LEAF), BF16),
            pltpu.VMEM((LEAF_DEV, NB, LEAF, LEAF), BF16),
            pltpu.VMEM((LEAF_DEV, R, LEAF), BF16),
            pltpu.VMEM((LEAF_DEV, R, R), BF16),
            pltpu.VMEM((LEAF_DEV, K_FAR, R, R), BF16),
            pltpu.VMEM((R, R, 2 * NDEV), F32),
            pltpu.VMEM((R, R, 2 * NDEV), F32),
            pltpu.VMEM((64, VEC, LEAF), BF16),
            pltpu.VMEM((64, VEC, LEAF), BF16),
            pltpu.VMEM((9, PAIRS, VEC, 2 * R), BF16),
            pltpu.VMEM((1024, VEC, 2 * R), BF16),
            pltpu.VMEM((48 * R, 2 * R), F32),
            pltpu.VMEM((16 * R, 2 * R), F32),
            pltpu.VMEM((3, HALF, 2 * R), F32),
            pltpu.VMEM((GY, HALF, 2 * R), F32),
            pltpu.VMEM((GX, HALF, 2 * R), F32),
            pltpu.VMEM((LEAF_DEV, VEC, LEAF), F32),
            pltpu.VMEM((LEAF_DEV, VEC, R), F32),
            pltpu.VMEM((4, R, 2 * R), BF16),
            pltpu.SMEM((NB, LEAF_DEV), jnp.int32),
            pltpu.SMEM((LEAF_DEV, K_FAR), jnp.int32),
            pltpu.SemaphoreType.DMA((10,)),
            pltpu.SemaphoreType.DMA((40,)),
            pltpu.SemaphoreType.DMA((40,)),
        ],
        compiler_params=pltpu.CompilerParams(
            collective_id=0, has_side_effects=True, vmem_limit_bytes=60 << 20
        ),
        cost_estimate=pl.CostEstimate(flops=600_000_000, bytes_accessed=29_000_000, transcendentals=0),
    )(
        vectors,
        near_tiles,
        near_list.T,
        leaf_basis,
        leaf_transfer,
        far_coupling,
        far_list,
        jnp.transpose(top_transfer, (1, 2, 0)),
        jnp.transpose(top_coupling, (1, 2, 0)),
    )


def solution(mesh):
    placed = (
        P(None, ("gx", "gy")),
        P(("gx", "gy"), None, None, None),
        P(("gx", "gy"), None),
        P(("gx", "gy"), None, None),
        P(("gx", "gy"), None, None),
        P(("gx", "gy"), None, None, None),
        P(("gx", "gy"), None),
        P(),
        P(),
    )
    return jax.shard_map(
        per_device, mesh=mesh, in_specs=placed, out_specs=P(None, ("gx", "gy")), check_vma=False
    )
```
